32 devices in a mesh: section: 4 (over y, core), dp: 8 (over z, x).
Axes of the slice: x: 2, y: 2, z: 4, core: 2. Of those that a mesh axis runs over, the one named last changes fastest.
Arguments:
- hidden_in: bfloat16 [4, 256, 8192], P(None, 'dp'), may hold values from -6 to 6
- cotangent: bfloat16 [4, 256, 8192], P(None, 'dp'), may hold values from -6 to 6
- adapter_in: bfloat16 [4, 8192, 128], P('section', 'dp'), may hold values from -0.0625 to 0.0625
- adapter_out: bfloat16 [4, 128, 8192], P('section', None, 'dp'), may hold values from -0.5 to 0.5
- norm_gain: bfloat16 [4, 8192], P('section', 'dp'), may hold values from 0.5 to 1.5
- user_of_row: int32 [4, 256], P(None, 'dp'), may hold values from 0 to 15, as said below
- included: int32 [4, 16], P(None, 'dp'), may hold values 0 or 1
Outputs:
- grad_in: float32 [4, 8192, 128], P('section', 'dp')
- grad_out: float32 [4, 128, 8192], P('section', None, 'dp')
- user_weights: float32 [4, 16], P(None, 'dp')
The draws below stay inside these ranges and needn't reach their ends.
Inputs may be any that keep to these rules, and one draw needn't show every extreme that they name: `user_of_row`: within one micro-batch, the rows of the j-th block of 32 rows belong to users j * 2 to j * 2 + 1, in rising order, each of them with one row or more.
All inputs are finite; a program needn't handle non-finite values. No bound on the sum of `included` on one device may be relied on, other than what follows from the above.
Results may differ from the reference program's by a relative error of at most 0.018.
Values may be sent and summed in bfloat16 or wider, within the bound.
No kernel may reach another device: no remote copies, remote signals or barrier semaphores. Data moves between devices by JAX's collectives and lax.ppermute only.
A program may use at most 64 MiB of HBM per device.

```python
import math
import jax
import jax.numpy as jnp
from jax import lax

D = 8192
RANK = 128
ROWS = 32
USERS_DEV = 2
MICRO = 4
LAYERS = 4
USERS = 16
N_SECTION = 4
N_DP = 8


def draw_user_of_row(key, part):
    scores = jax.random.randint(key, (MICRO, N_DP, ROWS - 1), 0, 1 << 20)
    scores = scores * ROWS + jnp.arange(ROWS - 1, dtype=jnp.int32)[None, None, :]
    unused, picked = lax.top_k(scores, USERS_DEV - 1)
    cuts = picked + 1
    places = jnp.arange(ROWS, dtype=jnp.int32)
    local = jnp.sum((cuts[:, :, None, :] <= places[None, None, :, None]).astype(jnp.int32), -1)
    owners = local + (jnp.arange(N_DP, dtype=jnp.int32) * USERS_DEV)[None, :, None]
    return owners.reshape(MICRO, N_DP * ROWS).astype(jnp.int32)


def block_rows(key):
    noise_key, shared_key, weight_key = jax.random.split(key, 3)
    noise = jax.random.normal(noise_key, (MICRO, N_DP, ROWS, D), jnp.float32)
    shared = jax.random.normal(shared_key, (MICRO, N_DP, 1, D), jnp.float32)
    weight = jax.random.uniform(weight_key, (MICRO, N_DP, ROWS, 1), jnp.float32, 0.8, 1.2)
    values = jnp.clip(noise + weight * shared, -6.0, 6.0)
    return values.reshape(MICRO, N_DP * ROWS, D).astype(jnp.bfloat16)


def draw_hidden_in(key, part):
    return block_rows(jax.random.fold_in(key, 11))


def draw_cotangent(key, part):
    return block_rows(jax.random.fold_in(key, 23))


def touch_ends(array, key, least, largest):
    longest = array.shape.index(max(array.shape))
    spots = []
    for shift in (0, 1):
        where = [jax.random.randint(jax.random.fold_in(key, axis), (), 0, length) for axis, length in enumerate(array.shape)]
        where[longest] = (where[longest] + shift) % array.shape[longest]
        spots.append(tuple(where))
    return array.at[spots[0]].set(least).at[spots[1]].set(largest)


def shard_levels(own_key, dims, pieces, least, top_value):
    def one(axis_at, shards_of):
        heights = jax.random.uniform(jax.random.fold_in(jax.random.fold_in(own_key, 6), axis_at), (shards_of,), jnp.float32, least / len(pieces), top_value / len(pieces))
        return jnp.repeat(jnp.exp(heights), dims[axis_at] // shards_of).reshape((-1,) + (1,) * (len(dims) - axis_at - 1))

    level = one(*pieces[0])
    for cut in pieces[1:]:
        level = level * one(*cut)
    return level


def gaussian(rng, dims, scale, most, cuts=(), held_as=jnp.bfloat16):
    values = jax.random.normal(rng, dims, jnp.float32) * scale
    if len(cuts) > 0:
        values = shard_levels(rng, dims, cuts, -0.22, 0.18) * values
    return jnp.clip(values, min=-most, max=most).astype(held_as)


def setup_inputs(seed: int = 0) -> dict:
    keys = jax.random.split(jax.random.key(seed), 8)
    return {
        "hidden_in": draw_hidden_in(jax.random.fold_in(keys[7], 71), 0),
        "cotangent": draw_cotangent(jax.random.fold_in(keys[7], 71), 0),
        "adapter_in": gaussian(keys[2], (LAYERS, D, RANK), D ** -0.5, 0.0625, ((0, 4), (1, 8))),
        "adapter_out": gaussian(keys[3], (LAYERS, RANK, D), RANK ** -0.5, 0.5, ((0, 4), (2, 8))),
        "norm_gain": jnp.clip(1.0 + 0.1 * jax.random.normal(keys[4], (LAYERS, D), jnp.float32), 0.5, 1.5).astype(jnp.bfloat16),
        "user_of_row": draw_user_of_row(jax.random.fold_in(keys[7], 71), 0),
        "included": touch_ends((jax.random.randint(keys[6], (MICRO, USERS), 0, 4) < 3).astype(jnp.int32), jax.random.fold_in(keys[6], 1), 0, 1),
    }


def normalize(stream_in, gain):
    stream = stream_in.astype(jnp.float32)
    scale = lax.rsqrt(lax.optimization_barrier(jnp.mean(stream * stream, -1, keepdims=True)) + 1e-05)
    unit = stream * scale
    normed = (unit * gain.astype(jnp.float32)).astype(jnp.bfloat16)
    return (stream, scale, unit, normed)

def flatten(values):
    return values.reshape(-1, values.shape[-1])

def pair_products(values):
    blocks = values.reshape(MICRO * N_DP, ROWS, values.shape[-1]).astype(jnp.float32)
    return jnp.einsum('bik,bjk->bij', blocks, blocks)

def ghost(normed, err, low, delta, user_of_row, onehot):
    owners = user_of_row.reshape(MICRO * N_DP, ROWS)
    same = owners[:, :, None] == owners[:, None, :]
    pairs = pair_products(normed) * pair_products(err) + pair_products(low) * pair_products(delta)
    pairs = jnp.where(same, pairs, jnp.zeros_like(pairs))
    rowsum = lax.optimization_barrier(jnp.sum(pairs, -1)).reshape(MICRO, N_DP * ROWS)
    return jnp.einsum('mr,mru->mu', rowsum, onehot)

def reference(hidden_in, cotangent, adapter_in, adapter_out, norm_gain, user_of_row, included):
    shape3 = hidden_in.shape
    onehot = (user_of_row[:, :, None] == jnp.arange(N_DP * USERS_DEV, dtype=jnp.int32)[None, None, :]).astype(jnp.float32)
    saved = []
    current = hidden_in
    for layer in range(N_SECTION):
        stream, scale, unit, normed = normalize(current, norm_gain[layer])
        low = jnp.dot(flatten(normed), adapter_in[layer], preferred_element_type=jnp.float32).astype(jnp.bfloat16)
        upper = jnp.dot(low, adapter_out[layer], preferred_element_type=jnp.float32).reshape(shape3)
        saved.append((current, normed, low.reshape(MICRO, N_DP * ROWS, RANK)))
        current = (stream + upper).astype(jnp.bfloat16)
    delta = cotangent
    total = jnp.zeros((MICRO, N_DP * USERS_DEV), jnp.float32)
    backs = [None] * N_SECTION
    for layer in range(N_SECTION - 1, -1, -1):
        entering, normed, low = saved[layer]
        stream, scale, unit, unused = normalize(entering, norm_gain[layer])
        err = jnp.dot(flatten(delta), adapter_out[layer].T, preferred_element_type=jnp.float32).astype(jnp.bfloat16)
        back = jnp.dot(err, adapter_in[layer].T, preferred_element_type=jnp.float32).reshape(shape3)
        slope = back * norm_gain[layer].astype(jnp.float32)
        grad_h = scale * (slope - unit * lax.optimization_barrier(jnp.mean(slope * unit, -1, keepdims=True)))
        err = err.reshape(MICRO, N_DP * ROWS, RANK)
        total = total + ghost(normed, err, low, delta, user_of_row, onehot)
        backs[layer] = (err, delta)
        delta = (delta.astype(jnp.float32) + grad_h).astype(jnp.bfloat16)
    bound = 0.8 * math.sqrt(N_SECTION * (ROWS // USERS_DEV) * D * D)
    user_weights = included.astype(jnp.float32) * (bound / jnp.maximum(jnp.sqrt(total), bound))
    row_weight = jnp.einsum('mru,mu->mr', onehot, user_weights)[:, :, None]
    grads_in = []
    grads_out = []
    for layer in range(N_SECTION):
        entering, normed, low = saved[layer]
        err, delta_next = backs[layer]
        weighted_err = (row_weight * err.astype(jnp.float32)).astype(jnp.bfloat16)
        weighted_delta = (row_weight * delta_next.astype(jnp.float32)).astype(jnp.bfloat16)
        grads_in.append(jnp.dot(flatten(normed).T, flatten(weighted_err), preferred_element_type=jnp.float32))
        grads_out.append(jnp.dot(flatten(low).T, flatten(weighted_delta), preferred_element_type=jnp.float32))
    return (jnp.stack(grads_in), jnp.stack(grads_out), user_weights)
```

```python
import functools
import math

import jax
import jax.numpy as jnp
from jax import lax
from jax.experimental import pallas as pl
from jax.experimental.pallas import tpu as pltpu
from jax.sharding import PartitionSpec as P

F32 = jnp.float32
BF16 = jnp.bfloat16
VMEM = pl.BlockSpec(memory_space=pltpu.VMEM)
SMEM = pl.BlockSpec(memory_space=pltpu.SMEM)
FAR = pl.BlockSpec(memory_space=pltpu.HBM)
ANY = pl.BlockSpec(memory_space=pl.ANY)
LIMIT = 16 * 1024 * 1024
LANES = 128
PAD = 16


def dot(left, right):
    return jnp.dot(left.astype(BF16), right.astype(BF16), preferred_element_type=F32)


def dot_last(left, right):
    return lax.dot_general(
        left.astype(BF16), right.astype(BF16), (((1,), (1,)), ((), ())), preferred_element_type=F32
    )


def dot_first(left, right):
    return lax.dot_general(
        left.astype(BF16), right.astype(BF16), (((0,), (0,)), ((), ())), preferred_element_type=F32
    )


def swap(block, axis, bit):
    size = lax.axis_size(axis)
    return lax.ppermute(block, axis, [(i, i ^ bit) for i in range(size)])


def exchange(blocks):
    return lax.all_to_all(blocks, "dp", 0, 0, tiled=True)


def out_in_vmem(shape, dtype):
    return pltpu.VMEM(shape, dtype)


def call(body, outs, specs, pinned=(), limit=LIMIT, **options):
    return pl.pallas_call(
        body,
        out_shape=[
            out_in_vmem(*out) if i in pinned else jax.ShapeDtypeStruct(*out)
            for i, out in enumerate(outs)
        ],
        in_specs=specs,
        out_specs=options.pop("out_specs", [VMEM] * len(outs)),
        compiler_params=pltpu.CompilerParams(vmem_limit_bytes=limit),
        **options,
    )


def in_hbm(*arrays):
    return [pltpu.with_memory_space_constraint(array, pltpu.HBM) for array in arrays]


def in_vmem(*arrays):
    return [pltpu.with_memory_space_constraint(array, pltpu.VMEM) for array in arrays]


def down_of(packs, layer, slab):
    return packs[layer, slab : 2 * slab, :]


def unchunk(block):
    rank = block.shape[1]
    return jnp.concatenate(
        [block[c * rank : (c + 1) * rank] for c in range(block.shape[0] // rank)], 1
    )


def up_of(packs, layer, slab):
    return unchunk(packs[layer, :slab, :])


def gain_of(packs, layer, slab):
    rank = packs.shape[2]
    rows = packs[layer, 2 * slab : 2 * slab + PAD, :].astype(F32)
    return jnp.concatenate([rows[c : c + 1, :] for c in range(slab // rank)], 1)


def first_micro(copies, share):
    return (lax.axis_index("section") // copies) * share


def split_kernel(copies, h_ref, c_ref, out_ref, sems):
    parts, _, own, slab = out_ref.shape
    rows = h_ref.shape[1]
    share = own // rows
    first = first_micro(copies, share)
    copies = []
    for i, whole in enumerate((h_ref, c_ref)):
        for n in range(parts):
            for m in range(share):
                copy = pltpu.make_async_copy(
                    whole.at[first + m, :, pl.ds(n * slab, slab)],
                    out_ref.at[n, i, pl.ds(m * rows, rows), :],
                    sems.at[i, n, m],
                )
                copy.start()
                copies.append(copy)
    for copy in copies:
        copy.wait()


def pack_kernel(down_ref, up_ref, gain_ref, up_out, down_out):
    slab, rank = down_ref.shape[1:]
    gain = gain_ref[...].astype(F32)
    parts = [gain[:, c * rank : (c + 1) * rank] for c in range(slab // rank)]
    for c, row in enumerate(parts):
        here = slice(c * rank, (c + 1) * rank)
        column = jnp.broadcast_to(row, (rank, rank)).T
        up_out[here, :] = up_ref[0, :, here]
        down_out[here, :] = (down_ref[0, here, :].astype(F32) * column).astype(BF16)
    spare = [jnp.zeros((PAD - len(parts), rank), F32)]
    down_out[slab:, :] = jnp.concatenate(parts + spare, 0).astype(BF16)


def products_kernel(down_ref, *refs):
    *pieces, gram_ref, ups_ref, sems = refs
    sections, slab, _ = ups_ref.shape
    rank = down_ref.shape[1]
    section = lax.axis_index("section")
    copies = [
        pltpu.make_async_copy(piece, ups_ref.at[section ^ offset], sems.at[i])
        for i, (piece, offset) in enumerate(zip(pieces, gathered_offsets(sections)))
    ]
    for copy in copies:
        copy.start()
    for copy in copies:
        copy.wait()
    own = unchunk(ups_ref[section])
    down = down_ref[:slab, :]
    for j in range(sections - 1):
        up = unchunk(ups_ref[j])
        value = jnp.where(j < section, dot(up, down), dot_last(own, up))
        gram_ref[j * rank : (j + 1) * rank, :] = value.astype(BF16)


def packs_kernel(*refs):
    *pieces, packs_ref, token_ref, sems = refs
    section = lax.axis_index("section")
    sections = packs_ref.shape[0]
    copies = []
    for i, offset in enumerate(gathered_offsets(sections)):
        begin = 0
        for j in range(2):
            piece = pieces[j * sections + i]
            target = packs_ref.at[section ^ offset, pl.ds(begin, piece.shape[0]), :]
            copies.append(pltpu.make_async_copy(piece, target, sems.at[j, i]))
            begin += piece.shape[0]
    for copy in copies:
        copy.start()
    token_ref[...] = jnp.zeros_like(token_ref)
    for copy in copies:
        copy.wait()


def gathered_offsets(sections, lowest=1):
    offsets = [0]
    bit = sections // 2
    while bit >= lowest:
        offsets = offsets + [offset ^ bit for offset in offsets]
        bit //= 2
    return offsets


def gather(block, lowest=1):
    pieces = gather_far(block, lowest)
    return pieces + [swap(piece, "section", lowest) for piece in pieces]


def gather_far(block, lowest):
    pieces = [block]
    bit = lax.axis_size("section") // 2
    while bit > lowest:
        pieces = pieces + [swap(piece, "section", bit) for piece in pieces]
        bit //= 2
    return pieces


def tie_kernel(block_ref, _, out_ref):
    del block_ref, out_ref


def add_tie_kernel(block_ref, sent_ref, came_ref, out_ref, sum_ref):
    del block_ref, out_ref
    sum_ref[...] = (sent_ref[...].astype(F32) + came_ref[...].astype(F32)).astype(BF16)


def add_tie(block, sent, came):
    return call(
        add_tie_kernel,
        [(block.shape, block.dtype), (sent.shape, sent.dtype)],
        [ANY, VMEM, VMEM],
        out_specs=[ANY, VMEM],
        input_output_aliases={0: 0},
    )(block, sent, came)


def tie(block, after):
    return call(
        tie_kernel,
        [(block.shape, block.dtype)],
        [ANY] * 2,
        out_specs=[ANY],
        input_output_aliases={0: 0},
    )(block, after)[0]


def notes_kernel(
    copies, slices_ref, h_ref, users_ref, included_ref, _, one_ref, two_ref, notes_ref, h_held, sem
):
    share, rows, _ = h_held.shape
    users = included_ref.shape[1]
    first = first_micro(copies, share)
    copy = pltpu.make_async_copy(h_ref.at[pl.ds(first, share)], h_held, sem)
    copy.start()
    cut = one_ref.shape[0]
    one_ref[...] = slices_ref[:cut]
    two_ref[...] = slices_ref[cut:]
    copy.wait()
    lane = lax.broadcasted_iota(jnp.int32, (rows, LANES), 1)
    diagonal = lax.broadcasted_iota(jnp.int32, (rows, rows), 0) == lax.broadcasted_iota(
        jnp.int32, (rows, rows), 1
    )
    for m in range(share):
        ids = users_ref[pl.ds(first + m, 1), :] - lax.axis_index("dp") * users
        column = jnp.sum(jnp.where(diagonal, ids, 0), -1, keepdims=True)
        wanted = included_ref[pl.ds(first + m, 1), :]
        chosen = jnp.zeros((rows, 1), jnp.int32)
        for u in range(users):
            chosen = chosen + jnp.where(column == u, wanted[:, u : u + 1], 0)
        wide = h_held[m].astype(F32)
        square = jnp.sum(wide * wide, -1, keepdims=True)
        notes = jnp.where(lane == 0, column.astype(F32), 0.0)
        notes = jnp.where(lane == 1, chosen.astype(F32), notes)
        notes_ref[m * rows : (m + 1) * rows, :] = jnp.where(lane == 2, square, notes)


def add_kernel(one_ref, two_ref, _, out_ref):
    out_ref[...] = (one_ref[...].astype(F32) + two_ref[...].astype(F32)).astype(BF16)


def project_kernel(slices_ref, packs_ref, _, out_ref):
    parts, _, own, slab = slices_ref.shape
    sections, _, rank = packs_ref.shape
    slice_h = slices_ref[:, 0].reshape(parts * own, slab)
    slice_c = slices_ref[:, 1].reshape(parts * own, slab)

    def put(value, index):
        here = slice(index * own, (index + 1) * own)
        out_ref[:, here, :] = value.astype(BF16).reshape(parts, own, rank)

    for l in range(sections):
        put(dot(slice_h, down_of(packs_ref, l, slab)), l)
    for l in range(sections):
        up = up_of(packs_ref, l, slab)
        put(dot_last(slice_c, up), 2 * sections - 1 + l)
        if l < sections - 1:
            put(dot_last(slice_h, up), sections + l)


def solve_kernel(width, notes_far, payload_ref, *refs):
    *pieces, out_ref, gram_ref, notes_ref, sems = refs
    pieces = pieces[3:]
    own = notes_ref.shape[0]
    parts, size, rank = out_ref.shape
    layers = (size // own - 1) // 2
    each = gram_ref.shape[0] // layers
    section = lax.axis_index("section")
    copies = [pltpu.make_async_copy(notes_far, notes_ref, sems.at[layers])]
    for i, (piece, offset) in enumerate(zip(pieces, gathered_offsets(layers))):
        begin = pl.multiple_of((section ^ offset) * each, each)
        copies.append(pltpu.make_async_copy(piece, gram_ref.at[pl.ds(begin, each), :], sems.at[i]))
    for copy in copies:
        copy.start()
    def column(index):
        return jnp.sum(payload_ref[:, index * own : (index + 1) * own, :].astype(F32), 0)

    def put(value, index):
        here = slice(index * own, (index + 1) * own)
        out_ref[:, here, :] = jnp.broadcast_to(value[None], (parts, own, rank))

    p = [column(i) for i in range(layers)]
    through = [column(layers + i) for i in range(layers - 1)]
    e = [column(2 * layers - 1 + i) for i in range(layers)]
    for copy in copies:
        copy.wait()
    gram = [
        [gram_ref[s * each + j * rank : s * each + (j + 1) * rank, :] for j in range(layers - 1)]
        for s in range(layers)
    ]
    square = notes_ref[:, 2:3]
    seen, low, exact, scale = [], [], [], []
    for l in range(layers):
        seen.append(list(through))
        scale.append(lax.rsqrt(jnp.maximum(square, 0.0) / width + 1e-05))
        exact.append(scale[l] * p[l])
        low.append(exact[l].astype(BF16))
        if l == layers - 1:
            break
        for k in range(l + 1, layers):
            p[k] = p[k] + dot(low[l], gram[k][l])
        before = through[l]
        for k in range(layers - 1):
            if k >= l:
                through[k] = through[k] + dot(low[l], gram[l][k])
            else:
                through[k] = through[k] + dot_last(low[l], gram[k][l])
        square = square + jnp.sum(low[l].astype(F32) * (before + through[l]), -1, keepdims=True)
    lane = lax.broadcasted_iota(jnp.int32, (own, rank), 1)
    extra = jnp.where(lane == 2 * layers, notes_ref[:, :1], 0.0)
    extra = jnp.where(lane == 2 * layers + 1, notes_ref[:, 1:2], extra)
    for l in range(layers - 1, -1, -1):
        err = e[l]
        mean = jnp.sum(err * exact[l], -1, keepdims=True) / width
        alpha = scale[l] * scale[l] * mean
        scaled = (scale[l] * err).astype(BF16)
        for k in range(l):
            e[k] = e[k] + dot_last(scaled, gram[l][k]) - alpha * seen[l][k]
        put(low[l], l)
        put(scaled, layers + l)
        coarse = alpha.astype(BF16).astype(F32)
        extra = jnp.where(lane == l, coarse, extra)
        extra = jnp.where(lane == layers + l, alpha - coarse, extra)
    put(extra.astype(BF16), 2 * layers)


def spread(extra, columns):
    rank = extra.shape[1]
    row = lax.broadcasted_iota(jnp.int32, (rank, rank), 0)
    picks = []
    for column in columns:
        pick = row == column[0]
        for other in column[1:]:
            pick = pick | (row == other)
        picks.append(jnp.where(pick, 1.0, 0.0).astype(BF16))
    wide = dot(extra, jnp.concatenate(picks, 1))
    return [wide[:, i * rank : (i + 1) * rank] for i in range(len(columns))]


def tiled(block, width):
    return jnp.concatenate([block] * (width // block.shape[1]), 1)


def place_of(counts, dimension, lanes):
    rows = math.prod(counts)
    return lax.broadcasted_iota(jnp.int32, counts + (lanes,), dimension).reshape(rows, lanes)


def user_lanes(ids, counts, users, lanes, m):
    lane = lax.broadcasted_iota(jnp.int32, (ids.shape[0], lanes), 1)
    user = tiled(ids, lanes).astype(jnp.int32) + place_of(counts, 0, lanes) * users
    mine = lane == user
    return mine if counts[1] == 1 else mine & (place_of(counts, 1, lanes) == m)


def state_rows(ref, index, own):
    parts, _, rank = ref.shape
    return ref[:, index * own : (index + 1) * own, :].reshape(parts * own, rank)


def streams_kernel(
    rows, users, slices_ref, packs_ref, states_ref, ghosts_ref, passed_ref, streams_ref, sem
):
    parts, _, own, slab = slices_ref.shape
    layers, _, rank = packs_ref.shape
    everyone = parts * own
    counts = (parts, own // rows, rows)
    passing = pltpu.make_async_copy(states_ref, passed_ref, sem)
    passing.start()

    def state(index):
        return state_rows(states_ref, index, own)

    extra = state(2 * layers)
    columns = [(2 * layers,)] + [(l, layers + l) for l in range(1, layers)]
    ids, *alphas = spread(extra, columns)
    step = rows
    while step < 256 and everyone % (2 * step) == 0:
        step *= 2
    spans = [slice(at, at + step) for at in range(0, everyone, step)]
    pairs = [jnp.zeros((step, step), F32) for _ in spans]
    stream = slices_ref[:, 0].reshape(everyone, slab)
    wide = stream.astype(F32)
    for l in range(layers):
        streams_ref[l] = stream
        low, scaled = state(l), state(layers + l)
        normed = (wide * gain_of(packs_ref, l, slab)).astype(BF16)
        for at, here in enumerate(spans):
            pairs[at] += dot_last(normed[here], normed[here]) * dot_last(scaled[here], scaled[here])
        if l < layers - 1:
            wide = wide + dot(low, up_of(packs_ref, l, slab))
            stream = wide.astype(BF16)
    delta = slices_ref[:, 1].reshape(everyone, slab)
    wide = delta.astype(F32)
    for l in range(layers - 1, -1, -1):
        low = state(l)
        for at, here in enumerate(spans):
            pairs[at] += dot_last(low[here], low[here]) * dot_last(delta[here], delta[here])
        if l > 0:
            wide = wide + dot_last(state(layers + l), down_of(packs_ref, l, slab))
            wide = wide - tiled(alphas[l - 1], slab) * streams_ref[l].astype(F32)
            delta = wide.astype(BF16)
    block = place_of((everyone // rows, rows), 0, rank).astype(F32)
    numbers = ids + block * users
    rowsums = []
    for at, here in enumerate(spans):
        number = numbers[here]
        other = jnp.transpose(number)[:1, :]
        own_number = tiled(number, step) if step >= rank else number[:, :step]
        rowsums.append(
            jnp.sum(jnp.where(own_number == other, pairs[at], 0.0), -1, keepdims=True)
        )
    rowsum = jnp.concatenate(rowsums, 0)
    copies, share, lanes = ghosts_ref.shape
    for m in range(share):
        mine = user_lanes(ids, counts, users, lanes, m)
        total = jnp.sum(jnp.where(mine, rowsum, 0.0), 0, keepdims=True)
        ghosts_ref[:, m : m + 1, :] = jnp.broadcast_to(total[None], (copies, 1, lanes))
    passing.wait()


def grads_kernel(rows, users, bound, copies, packs_ref, *refs):
    count = (len(refs) - 12) // 3
    one_pieces, two_pieces, state_pieces = (refs[i * count : (i + 1) * count] for i in range(3))
    (
        ghosts_ref,
        included_ref,
        in_ref,
        out_ref,
        weights_ref,
        h_held,
        c_held,
        state_held,
        clips_ref,
        h_sum,
        c_sum,
        sems,
    ) = refs[3 * count :]
    layers, _, rank = packs_ref.shape
    _, parts, own, slab = h_held.shape
    cut = one_pieces[0].shape[0]
    everyone = parts * own
    share, lanes = ghosts_ref.shape[2:]
    section = lax.axis_index("section")
    offsets = gathered_offsets(layers, copies)

    def moves(at, entry):
        one, two = pl.ds(0, cut), pl.ds(cut, parts - cut)
        return [
            pltpu.make_async_copy(state_pieces[entry], state_held.at[at], sems.at[at, 0]),
            pltpu.make_async_copy(one_pieces[entry].at[:, 0], h_held.at[at, one], sems.at[at, 1]),
            pltpu.make_async_copy(two_pieces[entry].at[:, 0], h_held.at[at, two], sems.at[at, 2]),
            pltpu.make_async_copy(one_pieces[entry].at[:, 1], c_held.at[at, one], sems.at[at, 3]),
            pltpu.make_async_copy(two_pieces[entry].at[:, 1], c_held.at[at, two], sems.at[at, 4]),
        ]

    for entry in range(count):
        for move in moves(entry, entry):
            move.start()
    h_sum[...] = jnp.zeros_like(h_sum)
    c_sum[...] = jnp.zeros_like(c_sum)
    columns = [(2 * layers,), (2 * layers + 1,)]
    for k in range(1, layers):
        taken = [jnp.where(l > section, l, -1) for l in range(k, layers)]
        columns.append(taken + [jnp.where(l >= 0, layers + l, -1) for l in taken])
    group = max(1, min(count, 512 // everyone))

    @pl.loop(0, count // group)
    def _(step):
        begin = step * group
        scaled, low, rest = [], [], [[] for _ in range(layers - 1)]
        for i in range(group):
            at = begin + i
            for move in moves(at, 0):
                move.wait()
            offset = sum(jnp.where(at == n, value, 0) for n, value in enumerate(offsets))
            there = section ^ offset
            totals = sum(ghosts_ref[there, n] for n in range(parts))
            clips = bound / jnp.maximum(jnp.sqrt(totals), bound)
            clips_ref[pl.ds((there // copies) * share, share), :] = clips
            state_ref = state_held.at[at]
            ids, included, *alphas = spread(state_rows(state_ref, 2 * layers, own), columns)
            weight = jnp.zeros((everyone, 1), F32)
            for m in range(share):
                mine = user_lanes(ids, (parts, share, rows), users, lanes, m)
                weight += jnp.sum(jnp.where(mine, clips[m : m + 1, :], 0.0), -1, keepdims=True)
            weight = weight * included

            def weighted(index):
                first = pl.multiple_of(index * own, own)
                block = state_ref[:, pl.ds(first, own), :].reshape(everyone, rank)
                return weight * block.astype(F32)

            scaled.append(weighted(layers + section).astype(BF16))
            low.append(weighted(section))
            for k in range(layers - 1):
                rest[k].append((alphas[k] * low[i]).astype(BF16))
        here = pl.ds(begin, group)

        def everything(ref, *index):
            return ref[(here,) + index].reshape(group * everyone, -1)

        def known(index):
            return everything(state_held, slice(None), slice(index * own, (index + 1) * own))

        scaled = jnp.concatenate(scaled, 0)
        low = jnp.concatenate(low, 0).astype(BF16)
        for k in range(layers - 1):
            sides = jnp.concatenate([scaled, jnp.concatenate(rest[k], 0)], 1)
            if k == 0:
                h_sum[:, :slab] += dot_first(sides, everything(h_held))
            h_sum[:, slab + k * rank : slab + (k + 1) * rank] += dot_first(sides, known(k))
        c_sum[:, :slab] += dot_first(low, everything(c_held))
        errs = jnp.concatenate([known(layers + k) for k in range(layers)], 1)
        c_sum[:, slab:] += dot_first(low, errs)

    left, right = h_sum[:rank, :slab], c_sum[:, :slab] - h_sum[rank:, :slab]
    for k in range(layers):
        beside = slice(slab + k * rank, slab + (k + 1) * rank)
        later = (k > section).astype(F32)
        right += dot_last(later * c_sum[:, beside], down_of(packs_ref, k, slab))
        if k < layers - 1:
            up = up_of(packs_ref, k, slab)
            earlier = (k < section).astype(F32)
            left += dot(earlier * h_sum[:rank, beside], up)
            right -= dot(h_sum[rank:, beside], up)
    out_ref[0] = right
    left = left * gain_of(packs_ref, section, slab)
    for c in range(slab // rank):
        part = slice(c * rank, (c + 1) * rank)
        in_ref[0, part, :] = left[:, part].T
    users_here, micro = included_ref.shape
    mine = lax.broadcasted_iota(jnp.int32, (micro, lanes), 1) - lax.axis_index("dp") * users
    diagonal = lax.broadcasted_iota(jnp.int32, (micro, micro), 0) == lax.broadcasted_iota(
        jnp.int32, (micro, micro), 1
    )
    for u in range(users_here):
        column = jnp.sum(jnp.where(mine == u, clips_ref[...], 0.0), -1, keepdims=True)
        row = jnp.sum(jnp.where(diagonal, column, 0.0), 0, keepdims=True)
        weights_ref[u : u + 1, :] = included_ref[u : u + 1, :].astype(F32) * row


def sum_parts(value, token):
    size = lax.axis_size("dp")
    bits = [1 << i for i in range(1, size.bit_length() - 1)]
    for bit in bits:
        came = swap(value, "dp", bit)
        if bit != bits[-1]:
            value = (value.astype(F32) + came.astype(F32)).astype(BF16)
        else:
            (value,) = call(add_kernel, [(value.shape, BF16)], [VMEM] * 3)(value, came, token)
    return value, swap(value, "dp", 1)


def shards(hidden_in, cotangent, adapter_in, adapter_out, norm_gain, user_of_row, included):
    sections = lax.axis_size("section")
    section = lax.axis_index("section")
    parts = lax.axis_size("dp")
    dp_index = lax.axis_index("dp")
    micro, rows, width = hidden_in.shape
    rank = adapter_in.shape[2]
    users = included.shape[1]
    layers = sections
    slab = width // parts
    share = max(1, micro // sections)
    copies = max(1, sections // micro)
    own = share * rows
    everyone = parts * own

    up, down = call(
        pack_kernel, [((slab, rank), BF16), ((slab + PAD, rank), BF16)], [VMEM] * 3
    )(*in_hbm(adapter_in, adapter_out, norm_gain))
    ups = gather(up)
    downs = gather(down)
    (blocks,) = call(
        functools.partial(split_kernel, copies),
        [((parts, 2, own, slab), BF16)],
        [FAR, FAR],
        scratch_shapes=[pltpu.SemaphoreType.DMA((2, parts, share))],
    )(*in_hbm(hidden_in, cotangent))
    slices = exchange(blocks)

    each = (layers - 1) * rank
    (gram,) = call(
        products_kernel,
        [((each, rank), BF16)],
        [VMEM, FAR] + [ANY] * (sections - 1),
        scratch_shapes=[
            pltpu.VMEM((sections, slab, rank), BF16),
            pltpu.SemaphoreType.DMA((sections,)),
        ],
    )(down, *in_hbm(up), *ups[1:])
    packs, token = call(
        packs_kernel,
        [((sections, 2 * slab + PAD, rank), BF16), ((8, LANES), F32)],
        [FAR] * (2 * sections),
        pinned=(0,),
        scratch_shapes=[pltpu.SemaphoreType.DMA((2, sections))],
    )(*in_hbm(*ups, *downs))
    sent, came = sum_parts(gram, token)

    (payload,) = call(
        project_kernel,
        [((parts, (3 * layers - 1) * own, rank), BF16)],
        [VMEM, VMEM, ANY],
    )(slices, *in_vmem(packs), sent)
    payload, gram = add_tie(payload, sent, came)
    payload = exchange(payload)
    grams = gather(gram)
    cut = max(1, parts * 2 // 8)
    one, two, notes = call(
        functools.partial(notes_kernel, copies),
        [
            ((cut, 2, own, slab), BF16),
            ((parts - cut, 2, own, slab), BF16),
            ((own, LANES), F32),
        ],
        [VMEM, FAR, VMEM, VMEM, ANY],
        scratch_shapes=[pltpu.VMEM((share, rows, width), BF16), pltpu.SemaphoreType.DMA],
    )(slices, *in_hbm(hidden_in), user_of_row, included, grams[1])
    ones = gather_far(one, copies)
    twos = gather_far(two, copies)
    ones_own, twos_own = swap(one, "section", copies), swap(two, "section", copies)
    count = 2 * len(ones)

    (state,) = call(
        functools.partial(solve_kernel, width),
        [((parts, (2 * layers + 1) * own, rank), BF16)],
        [FAR, VMEM] + [FAR] * (3 + len(grams)),
        scratch_shapes=[
            pltpu.VMEM((layers * each, rank), BF16),
            pltpu.VMEM((own, LANES), F32),
            pltpu.SemaphoreType.DMA((layers + 1,)),
        ],
    )(*in_hbm(notes), payload, *in_hbm(ones[1], ones_own, twos_own, *grams))
    states = exchange(state)

    lanes = -(-users * parts // LANES) * LANES
    ghosts, mine = call(
        functools.partial(streams_kernel, rows, users),
        [((sections * parts, share, lanes), F32), (states.shape, BF16)],
        [VMEM] * 3,
        out_specs=[VMEM, FAR],
        scratch_shapes=[
            pltpu.VMEM((layers, everyone, slab), BF16),
            pltpu.SemaphoreType.DMA,
        ],
    )(slices, *in_vmem(packs), states)
    states_far = gather_far(states, copies)
    ghosts = lax.all_to_all(ghosts, ("section", "dp"), 0, 0, tiled=True)
    ones = ones[:1] + [tie(piece, ghosts) for piece in ones[1:]]
    twos = twos[:1] + [tie(piece, ghosts) for piece in twos[1:]]
    ones = ones + [ones_own] + [swap(piece, "section", copies) for piece in ones[1:]]
    twos = twos + [twos_own] + [swap(piece, "section", copies) for piece in twos[1:]]
    states = [tie(mine, ghosts)] + [tie(piece, ghosts) for piece in states_far[1:]]
    states = states + [swap(piece, "section", copies) for piece in states]
    ghosts = ghosts.reshape(sections, parts, share, lanes)
    bound = 0.8 * math.sqrt(sections * (rows // users) * width * width)

    grad_in, grad_out, weights = call(
        functools.partial(grads_kernel, rows, users, bound, copies),
        [((1, slab, rank), F32), ((1, rank, slab), F32), ((users, micro), F32)],
        [VMEM] + [FAR] * (2 * count + 1) + [ANY] * (count - 1) + [VMEM] * 2,
        limit=LIMIT + 3 * count * (states[0].size + slices.size),
        scratch_shapes=[
            pltpu.VMEM((count, parts, own, slab), BF16),
            pltpu.VMEM((count, parts, own, slab), BF16),
            pltpu.VMEM((count,) + states[0].shape, BF16),
            pltpu.VMEM((micro, lanes), F32),
            pltpu.VMEM((2 * rank, slab + (layers - 1) * rank), F32),
            pltpu.VMEM((rank, slab + layers * rank), F32),
            pltpu.SemaphoreType.DMA((count, 5)),
        ],
    )(
        *in_vmem(packs),
        *in_hbm(*ones, *twos, states[0]),
        *states[1:],
        ghosts,
        included.T,
    )
    return (grad_in, grad_out, weights.T)


def solution(mesh):
    placed = (
        P(None, "dp", None),
        P(None, "dp", None),
        P("section", "dp", None),
        P("section", None, "dp"),
        P("section", "dp"),
        P(None, "dp"),
        P(None, "dp"),
    )
    return jax.shard_map(
        shards,
        mesh=mesh,
        in_specs=placed,
        out_specs=(P("section", "dp", None), P("section", None, "dp"), P(None, "dp")),
        check_vma=False,
    )
```

```python
import functools
import math

import jax
import jax.numpy as jnp
from jax import lax
from jax.experimental import pallas as pl
from jax.experimental.pallas import tpu as pltpu
from jax.sharding import PartitionSpec as P

F32 = jnp.float32
BF16 = jnp.bfloat16
VMEM = pl.BlockSpec(memory_space=pltpu.VMEM)
SMEM = pl.BlockSpec(memory_space=pltpu.SMEM)
FAR = pl.BlockSpec(memory_space=pltpu.HBM)
ANY = pl.BlockSpec(memory_space=pl.ANY)
LIMIT = 16 * 1024 * 1024
LANES = 128
PAD = 16


def dot(left, right):
    return jnp.dot(left.astype(BF16), right.astype(BF16), preferred_element_type=F32)


def dot_last(left, right):
    return lax.dot_general(
        left.astype(BF16), right.astype(BF16), (((1,), (1,)), ((), ())), preferred_element_type=F32
    )


def dot_first(left, right):
    return lax.dot_general(
        left.astype(BF16), right.astype(BF16), (((0,), (0,)), ((), ())), preferred_element_type=F32
    )


def swap(block, axis, bit):
    size = lax.axis_size(axis)
    return lax.ppermute(block, axis, [(i, i ^ bit) for i in range(size)])


def exchange(blocks):
    return lax.all_to_all(blocks, "dp", 0, 0, tiled=True)


def out_in_vmem(shape, dtype):
    return pltpu.VMEM(shape, dtype)


def call(body, outs, specs, pinned=(), limit=LIMIT, **options):
    return pl.pallas_call(
        body,
        out_shape=[
            out_in_vmem(*out) if i in pinned else jax.ShapeDtypeStruct(*out)
            for i, out in enumerate(outs)
        ],
        in_specs=specs,
        out_specs=options.pop("out_specs", [VMEM] * len(outs)),
        compiler_params=pltpu.CompilerParams(vmem_limit_bytes=limit),
        **options,
    )


def in_hbm(*arrays):
    return [pltpu.with_memory_space_constraint(array, pltpu.HBM) for array in arrays]


def in_vmem(*arrays):
    return [pltpu.with_memory_space_constraint(array, pltpu.VMEM) for array in arrays]


def down_of(packs, layer, slab):
    return packs[layer, slab : 2 * slab, :]


def unchunk(block):
    rank = block.shape[1]
    return jnp.concatenate(
        [block[c * rank : (c + 1) * rank] for c in range(block.shape[0] // rank)], 1
    )


def up_of(packs, layer, slab):
    return unchunk(packs[layer, :slab, :])


def gain_of(packs, layer, slab):
    rank = packs.shape[2]
    rows = packs[layer, 2 * slab : 2 * slab + PAD, :].astype(F32)
    return jnp.concatenate([rows[c : c + 1, :] for c in range(slab // rank)], 1)


def first_micro(copies, share):
    return (lax.axis_index("section") // copies) * share


def split_kernel(copies, h_ref, c_ref, out_ref, sems):
    parts, _, own, slab = out_ref.shape
    rows = h_ref.shape[1]
    share = own // rows
    first = first_micro(copies, share)
    copies = []
    for i, whole in enumerate((h_ref, c_ref)):
        for n in range(parts):
            for m in range(share):
                copy = pltpu.make_async_copy(
                    whole.at[first + m, :, pl.ds(n * slab, slab)],
                    out_ref.at[n, i, pl.ds(m * rows, rows), :],
                    sems.at[i, n, m],
                )
                copy.start()
                copies.append(copy)
    for copy in copies:
        copy.wait()


def pack_kernel(down_ref, up_ref, gain_ref, up_out, down_out):
    slab, rank = down_ref.shape[1:]
    gain = gain_ref[...].astype(F32)
    parts = [gain[:, c * rank : (c + 1) * rank] for c in range(slab // rank)]
    for c, row in enumerate(parts):
        here = slice(c * rank, (c + 1) * rank)
        column = jnp.broadcast_to(row, (rank, rank)).T
        up_out[here, :] = up_ref[0, :, here]
        down_out[here, :] = (down_ref[0, here, :].astype(F32) * column).astype(BF16)
    spare = [jnp.zeros((PAD - len(parts), rank), F32)]
    down_out[slab:, :] = jnp.concatenate(parts + spare, 0).astype(BF16)


def products_kernel(down_ref, *refs):
    *pieces, gram_ref, ups_ref, sems = refs
    sections, slab, _ = ups_ref.shape
    rank = down_ref.shape[1]
    section = lax.axis_index("section")
    copies = [
        pltpu.make_async_copy(piece, ups_ref.at[section ^ offset], sems.at[i])
        for i, (piece, offset) in enumerate(zip(pieces, gathered_offsets(sections)))
    ]
    for copy in copies:
        copy.start()
    for copy in copies:
        copy.wait()
    own = unchunk(ups_ref[section])
    down = down_ref[:slab, :]
    for j in range(sections - 1):
        up = unchunk(ups_ref[j])
        value = jnp.where(j < section, dot(up, down), dot_last(own, up))
        gram_ref[j * rank : (j + 1) * rank, :] = value.astype(BF16)


def packs_kernel(*refs):
    *pieces, packs_ref, token_ref, sems = refs
    section = lax.axis_index("section")
    sections = packs_ref.shape[0]
    copies = []
    for i, offset in enumerate(gathered_offsets(sections)):
        begin = 0
        for j in range(2):
            piece = pieces[j * sections + i]
            target = packs_ref.at[section ^ offset, pl.ds(begin, piece.shape[0]), :]
            copies.append(pltpu.make_async_copy(piece, target, sems.at[j, i]))
            begin += piece.shape[0]
    for copy in copies:
        copy.start()
    token_ref[...] = jnp.zeros_like(token_ref)
    for copy in copies:
        copy.wait()


def gathered_offsets(sections, lowest=1):
    offsets = [0]
    bit = sections // 2
    while bit >= lowest:
        offsets = offsets + [offset ^ bit for offset in offsets]
        bit //= 2
    return offsets


def gather(block, lowest=1):
    pieces = gather_far(block, lowest)
    return pieces + [swap(piece, "section", lowest) for piece in pieces]


def gather_far(block, lowest):
    pieces = [block]
    bit = lax.axis_size("section") // 2
    while bit > lowest:
        pieces = pieces + [swap(piece, "section", bit) for piece in pieces]
        bit //= 2
    return pieces


def tie_kernel(block_ref, _, out_ref):
    del block_ref, out_ref


def tie(block, after):
    return call(
        tie_kernel,
        [(block.shape, block.dtype)],
        [ANY] * 2,
        out_specs=[ANY],
        input_output_aliases={0: 0},
    )(block, after)[0]


def notes_kernel(
    copies, slices_ref, h_ref, users_ref, included_ref, _, one_ref, two_ref, notes_ref, h_held, sem
):
    share, rows, _ = h_held.shape
    users = included_ref.shape[1]
    first = first_micro(copies, share)
    copy = pltpu.make_async_copy(h_ref.at[pl.ds(first, share)], h_held, sem)
    copy.start()
    cut = one_ref.shape[0]
    one_ref[...] = slices_ref[:cut]
    two_ref[...] = slices_ref[cut:]
    copy.wait()
    lane = lax.broadcasted_iota(jnp.int32, (rows, LANES), 1)
    diagonal = lax.broadcasted_iota(jnp.int32, (rows, rows), 0) == lax.broadcasted_iota(
        jnp.int32, (rows, rows), 1
    )
    for m in range(share):
        ids = users_ref[pl.ds(first + m, 1), :] - lax.axis_index("dp") * users
        column = jnp.sum(jnp.where(diagonal, ids, 0), -1, keepdims=True)
        wanted = included_ref[pl.ds(first + m, 1), :]
        chosen = jnp.zeros((rows, 1), jnp.int32)
        for u in range(users):
            chosen = chosen + jnp.where(column == u, wanted[:, u : u + 1], 0)
        wide = h_held[m].astype(F32)
        square = jnp.sum(wide * wide, -1, keepdims=True)
        notes = jnp.where(lane == 0, column.astype(F32), 0.0)
        notes = jnp.where(lane == 1, chosen.astype(F32), notes)
        notes_ref[m * rows : (m + 1) * rows, :] = jnp.where(lane == 2, square, notes)


def add_kernel(one_ref, two_ref, _, out_ref):
    out_ref[...] = (one_ref[...].astype(F32) + two_ref[...].astype(F32)).astype(BF16)


def project_kernel(slices_ref, packs_ref, _, out_ref, token_ref):
    token_ref[...] = jnp.zeros_like(token_ref)
    parts, _, own, slab = slices_ref.shape
    sections, _, rank = packs_ref.shape
    slice_h = slices_ref[:, 0].reshape(parts * own, slab)
    slice_c = slices_ref[:, 1].reshape(parts * own, slab)

    def put(value, index):
        here = slice(index * own, (index + 1) * own)
        out_ref[:, here, :] = value.astype(BF16).reshape(parts, own, rank)

    for l in range(sections):
        put(dot(slice_h, down_of(packs_ref, l, slab)), l)
    for l in range(sections):
        up = up_of(packs_ref, l, slab)
        put(dot_last(slice_c, up), 2 * sections - 1 + l)
        if l < sections - 1:
            put(dot_last(slice_h, up), sections + l)


def solve_kernel(width, notes_far, payload_ref, *refs):
    *pieces, out_ref, gram_ref, notes_ref, sems = refs
    own = notes_ref.shape[0]
    parts, size, rank = out_ref.shape
    layers = (size // own - 1) // 2
    pieces = pieces[-layers:]
    each = gram_ref.shape[0] // layers
    section = lax.axis_index("section")
    copies = [pltpu.make_async_copy(notes_far, notes_ref, sems.at[layers])]
    for i, (piece, offset) in enumerate(zip(pieces, gathered_offsets(layers))):
        begin = pl.multiple_of((section ^ offset) * each, each)
        copies.append(pltpu.make_async_copy(piece, gram_ref.at[pl.ds(begin, each), :], sems.at[i]))
    for copy in copies:
        copy.start()
    def column(index):
        return jnp.sum(payload_ref[:, index * own : (index + 1) * own, :].astype(F32), 0)

    def put(value, index):
        here = slice(index * own, (index + 1) * own)
        out_ref[:, here, :] = jnp.broadcast_to(value[None], (parts, own, rank))

    p = [column(i) for i in range(layers)]
    through = [column(layers + i) for i in range(layers - 1)]
    e = [column(2 * layers - 1 + i) for i in range(layers)]
    for copy in copies:
        copy.wait()
    gram = [
        [gram_ref[s * each + j * rank : s * each + (j + 1) * rank, :] for j in range(layers - 1)]
        for s in range(layers)
    ]
    square = notes_ref[:, 2:3]
    seen, low, exact, scale = [], [], [], []
    for l in range(layers):
        seen.append(list(through))
        scale.append(lax.rsqrt(jnp.maximum(square, 0.0) / width + 1e-05))
        exact.append(scale[l] * p[l])
        low.append(exact[l].astype(BF16))
        if l == layers - 1:
            break
        for k in range(l + 1, layers):
            p[k] = p[k] + dot(low[l], gram[k][l])
        before = through[l]
        for k in range(layers - 1):
            if k >= l:
                through[k] = through[k] + dot(low[l], gram[l][k])
            else:
                through[k] = through[k] + dot_last(low[l], gram[k][l])
        square = square + jnp.sum(low[l].astype(F32) * (before + through[l]), -1, keepdims=True)
    lane = lax.broadcasted_iota(jnp.int32, (own, rank), 1)
    extra = jnp.where(lane == 2 * layers, notes_ref[:, :1], 0.0)
    extra = jnp.where(lane == 2 * layers + 1, notes_ref[:, 1:2], extra)
    for l in range(layers - 1, -1, -1):
        err = e[l]
        mean = jnp.sum(err * exact[l], -1, keepdims=True) / width
        alpha = scale[l] * scale[l] * mean
        scaled = (scale[l] * err).astype(BF16)
        for k in range(l):
            e[k] = e[k] + dot_last(scaled, gram[l][k]) - alpha * seen[l][k]
        put(low[l], l)
        put(scaled, layers + l)
        coarse = alpha.astype(BF16).astype(F32)
        extra = jnp.where(lane == l, coarse, extra)
        extra = jnp.where(lane == layers + l, alpha - coarse, extra)
    put(extra.astype(BF16), 2 * layers)


def spread(extra, columns):
    rank = extra.shape[1]
    row = lax.broadcasted_iota(jnp.int32, (rank, rank), 0)
    picks = []
    for column in columns:
        pick = row == column[0]
        for other in column[1:]:
            pick = pick | (row == other)
        picks.append(jnp.where(pick, 1.0, 0.0).astype(BF16))
    wide = dot(extra, jnp.concatenate(picks, 1))
    return [wide[:, i * rank : (i + 1) * rank] for i in range(len(columns))]


def tiled(block, width):
    return jnp.concatenate([block] * (width // block.shape[1]), 1)


def place_of(counts, dimension, lanes):
    rows = math.prod(counts)
    return lax.broadcasted_iota(jnp.int32, counts + (lanes,), dimension).reshape(rows, lanes)


def user_lanes(ids, counts, users, lanes, m):
    lane = lax.broadcasted_iota(jnp.int32, (ids.shape[0], lanes), 1)
    user = tiled(ids, lanes).astype(jnp.int32) + place_of(counts, 0, lanes) * users
    mine = lane == user
    return mine if counts[1] == 1 else mine & (place_of(counts, 1, lanes) == m)


def state_rows(ref, index, own):
    parts, _, rank = ref.shape
    return ref[:, index * own : (index + 1) * own, :].reshape(parts * own, rank)


def streams_kernel(
    rows, users, slices_ref, packs_ref, states_ref, ghosts_ref, streams_ref, held_ref, sems
):
    parts, _, own, slab = slices_ref.shape
    layers, _, rank = packs_ref.shape
    everyone = parts * own
    counts = (parts, own // rows, rows)
    halves = [pl.ds(0, layers * own), pl.ds(layers * own, (layers + 1) * own)]
    copies = [
        pltpu.make_async_copy(states_ref.at[:, half], held_ref.at[:, half], sems.at[i])
        for i, half in enumerate(halves)
    ]
    for copy in copies:
        copy.start()

    def state(index):
        return state_rows(held_ref, index, own)

    step = rows
    while step < 256 and everyone % (2 * step) == 0:
        step *= 2
    spans = [slice(at, at + step) for at in range(0, everyone, step)]
    pairs = [jnp.zeros((step, step), F32) for _ in spans]
    stream = slices_ref[:, 0].reshape(everyone, slab)
    wide = stream.astype(F32)
    for l in range(layers):
        streams_ref[l] = stream
        normed = (wide * gain_of(packs_ref, l, slab)).astype(BF16)
        grams = [dot_last(normed[here], normed[here]) for here in spans]
        if l == 0:
            for copy in copies:
                copy.wait()
        low, scaled = state(l), state(layers + l)
        for at, here in enumerate(spans):
            pairs[at] += grams[at] * dot_last(scaled[here], scaled[here])
        if l < layers - 1:
            wide = wide + dot(low, up_of(packs_ref, l, slab))
            stream = wide.astype(BF16)
    extra = state(2 * layers)
    columns = [(2 * layers,)] + [(l, layers + l) for l in range(1, layers)]
    ids, *alphas = spread(extra, columns)
    delta = slices_ref[:, 1].reshape(everyone, slab)
    wide = delta.astype(F32)
    for l in range(layers - 1, -1, -1):
        low = state(l)
        for at, here in enumerate(spans):
            pairs[at] += dot_last(low[here], low[here]) * dot_last(delta[here], delta[here])
        if l > 0:
            wide = wide + dot_last(state(layers + l), down_of(packs_ref, l, slab))
            wide = wide - tiled(alphas[l - 1], slab) * streams_ref[l].astype(F32)
            delta = wide.astype(BF16)
    block = place_of((everyone // rows, rows), 0, rank).astype(F32)
    numbers = ids + block * users
    rowsums = []
    for at, here in enumerate(spans):
        number = numbers[here]
        other = jnp.transpose(number)[:1, :]
        own_number = tiled(number, step) if step >= rank else number[:, :step]
        rowsums.append(
            jnp.sum(jnp.where(own_number == other, pairs[at], 0.0), -1, keepdims=True)
        )
    rowsum = jnp.concatenate(rowsums, 0)
    copies, share, lanes = ghosts_ref.shape
    for m in range(share):
        mine = user_lanes(ids, counts, users, lanes, m)
        total = jnp.sum(jnp.where(mine, rowsum, 0.0), 0, keepdims=True)
        ghosts_ref[:, m : m + 1, :] = jnp.broadcast_to(total[None], (copies, 1, lanes))

def grads_kernel(rows, users, bound, copies, packs_ref, *refs):
    count = (len(refs) - 12) // 3
    one_pieces, two_pieces, state_pieces = (refs[i * count : (i + 1) * count] for i in range(3))
    (
        ghosts_ref,
        included_ref,
        in_ref,
        out_ref,
        weights_ref,
        h_held,
        c_held,
        state_held,
        clips_ref,
        h_sum,
        c_sum,
        sems,
    ) = refs[3 * count :]
    layers, _, rank = packs_ref.shape
    _, parts, own, slab = h_held.shape
    cut = one_pieces[0].shape[0]
    everyone = parts * own
    share, lanes = ghosts_ref.shape[2:]
    section = lax.axis_index("section")
    offsets = gathered_offsets(layers, copies)

    def moves(at, entry):
        one, two = pl.ds(0, cut), pl.ds(cut, parts - cut)
        return [
            pltpu.make_async_copy(state_pieces[entry], state_held.at[at], sems.at[at, 0]),
            pltpu.make_async_copy(one_pieces[entry].at[:, 0], h_held.at[at, one], sems.at[at, 1]),
            pltpu.make_async_copy(two_pieces[entry].at[:, 0], h_held.at[at, two], sems.at[at, 2]),
            pltpu.make_async_copy(one_pieces[entry].at[:, 1], c_held.at[at, one], sems.at[at, 3]),
            pltpu.make_async_copy(two_pieces[entry].at[:, 1], c_held.at[at, two], sems.at[at, 4]),
        ]

    for entry in range(count):
        for move in moves(entry, entry):
            move.start()
    h_sum[...] = jnp.zeros_like(h_sum)
    c_sum[...] = jnp.zeros_like(c_sum)
    columns = [(2 * layers,), (2 * layers + 1,)]
    for k in range(1, layers):
        taken = [jnp.where(l > section, l, -1) for l in range(k, layers)]
        columns.append(taken + [jnp.where(l >= 0, layers + l, -1) for l in taken])
    group = max(1, min(count, 512 // everyone))

    @pl.loop(0, count // group)
    def _(step):
        begin = step * group
        scaled, low, rest = [], [], [[] for _ in range(layers - 1)]
        for i in range(group):
            at = begin + i
            for move in moves(at, 0):
                move.wait()
            offset = sum(jnp.where(at == n, value, 0) for n, value in enumerate(offsets))
            there = section ^ offset
            totals = sum(ghosts_ref[there, n] for n in range(parts))
            clips = bound / jnp.maximum(jnp.sqrt(totals), bound)
            clips_ref[pl.ds((there // copies) * share, share), :] = clips
            state_ref = state_held.at[at]
            ids, included, *alphas = spread(state_rows(state_ref, 2 * layers, own), columns)
            weight = jnp.zeros((everyone, 1), F32)
            for m in range(share):
                mine = user_lanes(ids, (parts, share, rows), users, lanes, m)
                weight += jnp.sum(jnp.where(mine, clips[m : m + 1, :], 0.0), -1, keepdims=True)
            weight = weight * included

            def weighted(index):
                first = pl.multiple_of(index * own, own)
                block = state_ref[:, pl.ds(first, own), :].reshape(everyone, rank)
                return weight * block.astype(F32)

            scaled.append(weighted(layers + section).astype(BF16))
            low.append(weighted(section))
            for k in range(layers - 1):
                rest[k].append((alphas[k] * low[i]).astype(BF16))
        here = pl.ds(begin, group)

        def everything(ref, *index):
            return ref[(here,) + index].reshape(group * everyone, -1)

        def known(index):
            return everything(state_held, slice(None), slice(index * own, (index + 1) * own))

        scaled = jnp.concatenate(scaled, 0)
        low = jnp.concatenate(low, 0).astype(BF16)
        for k in range(layers - 1):
            sides = jnp.concatenate([scaled, jnp.concatenate(rest[k], 0)], 1)
            if k == 0:
                h_sum[:, :slab] += dot_first(sides, everything(h_held))
            h_sum[:, slab + k * rank : slab + (k + 1) * rank] += dot_first(sides, known(k))
        c_sum[:, :slab] += dot_first(low, everything(c_held))
        errs = jnp.concatenate([known(layers + k) for k in range(layers)], 1)
        c_sum[:, slab:] += dot_first(low, errs)

    left, right = h_sum[:rank, :slab], c_sum[:, :slab] - h_sum[rank:, :slab]
    for k in range(layers):
        beside = slice(slab + k * rank, slab + (k + 1) * rank)
        later = (k > section).astype(F32)
        right += dot_last(later * c_sum[:, beside], down_of(packs_ref, k, slab))
        if k < layers - 1:
            up = up_of(packs_ref, k, slab)
            earlier = (k < section).astype(F32)
            left += dot(earlier * h_sum[:rank, beside], up)
            right -= dot(h_sum[rank:, beside], up)
    out_ref[0] = right
    left = left * gain_of(packs_ref, section, slab)
    for c in range(slab // rank):
        part = slice(c * rank, (c + 1) * rank)
        in_ref[0, part, :] = left[:, part].T
    users_here, micro = included_ref.shape
    mine = lax.broadcasted_iota(jnp.int32, (micro, lanes), 1) - lax.axis_index("dp") * users
    diagonal = lax.broadcasted_iota(jnp.int32, (micro, micro), 0) == lax.broadcasted_iota(
        jnp.int32, (micro, micro), 1
    )
    for u in range(users_here):
        column = jnp.sum(jnp.where(mine == u, clips_ref[...], 0.0), -1, keepdims=True)
        row = jnp.sum(jnp.where(diagonal, column, 0.0), 0, keepdims=True)
        weights_ref[u : u + 1, :] = included_ref[u : u + 1, :].astype(F32) * row


def sum_parts(value, token):
    size = lax.axis_size("dp")
    bits = [1 << i for i in range(1, size.bit_length() - 1)]
    for bit in bits:
        came = swap(value, "dp", bit)
        if bit != bits[-1]:
            value = (value.astype(F32) + came.astype(F32)).astype(BF16)
        else:
            (value,) = call(add_kernel, [(value.shape, BF16)], [VMEM] * 3)(value, came, token)
    return value, swap(value, "dp", 1)


def shards(hidden_in, cotangent, adapter_in, adapter_out, norm_gain, user_of_row, included):
    sections = lax.axis_size("section")
    section = lax.axis_index("section")
    parts = lax.axis_size("dp")
    dp_index = lax.axis_index("dp")
    micro, rows, width = hidden_in.shape
    rank = adapter_in.shape[2]
    users = included.shape[1]
    layers = sections
    slab = width // parts
    share = max(1, micro // sections)
    copies = max(1, sections // micro)
    own = share * rows
    everyone = parts * own

    up, down = call(
        pack_kernel, [((slab, rank), BF16), ((slab + PAD, rank), BF16)], [VMEM] * 3
    )(*in_hbm(adapter_in, adapter_out, norm_gain))
    ups = gather(up)
    downs = gather(down)
    (blocks,) = call(
        functools.partial(split_kernel, copies),
        [((parts, 2, own, slab), BF16)],
        [FAR, FAR],
        scratch_shapes=[pltpu.SemaphoreType.DMA((2, parts, share))],
    )(*in_hbm(hidden_in, cotangent))
    slices = exchange(blocks)

    each = (layers - 1) * rank
    (gram,) = call(
        products_kernel,
        [((each, rank), BF16)],
        [VMEM, FAR] + [ANY] * (sections - 1),
        scratch_shapes=[
            pltpu.VMEM((sections, slab, rank), BF16),
            pltpu.SemaphoreType.DMA((sections,)),
        ],
    )(down, *in_hbm(up), *ups[1:])
    packs, token = call(
        packs_kernel,
        [((sections, 2 * slab + PAD, rank), BF16), ((8, LANES), F32)],
        [FAR] * (2 * sections),
        pinned=(0,),
        scratch_shapes=[pltpu.SemaphoreType.DMA((2, sections))],
    )(*in_hbm(*ups, *downs))
    sent, came = sum_parts(gram, token)

    payload, token = call(
        project_kernel,
        [((parts, (3 * layers - 1) * own, rank), BF16), ((8, LANES), F32)],
        [VMEM, VMEM, ANY],
    )(slices, *in_vmem(packs), sent)
    payload = exchange(payload)
    gram = (sent.astype(F32) + came.astype(F32)).astype(BF16)
    grams = gather(gram)
    cut = max(1, parts * 3 // 8)
    one, two, notes = call(
        functools.partial(notes_kernel, copies),
        [
            ((cut, 2, own, slab), BF16),
            ((parts - cut, 2, own, slab), BF16),
            ((own, LANES), F32),
        ],
        [VMEM, FAR, VMEM, VMEM, VMEM],
        scratch_shapes=[pltpu.VMEM((share, rows, width), BF16), pltpu.SemaphoreType.DMA],
    )(slices, *in_hbm(hidden_in), user_of_row, included, token)
    ones = gather(one, copies)
    twos = gather_far(two, copies)
    twos_own = swap(two, "section", copies)
    count = len(ones)

    (state,) = call(
        functools.partial(solve_kernel, width),
        [((parts, (2 * layers + 1) * own, rank), BF16)],
        [FAR, VMEM] + [FAR] * (count + len(grams)),
        scratch_shapes=[
            pltpu.VMEM((layers * each, rank), BF16),
            pltpu.VMEM((own, LANES), F32),
            pltpu.SemaphoreType.DMA((layers + 1,)),
        ],
    )(*in_hbm(notes), payload, *in_hbm(*ones[1:], twos_own, *grams))
    states = exchange(state)

    lanes = -(-users * parts // LANES) * LANES
    (ghosts,) = call(
        functools.partial(streams_kernel, rows, users),
        [((sections * parts, share, lanes), F32)],
        [VMEM, VMEM, FAR],
        limit=LIMIT + 4 * states.size,
        scratch_shapes=[
            pltpu.VMEM((layers, everyone, slab), BF16),
            pltpu.VMEM(states.shape, BF16),
            pltpu.SemaphoreType.DMA((2,)),
        ],
    )(slices, *in_vmem(packs), *in_hbm(states))
    states_far = gather_far(states, copies)
    ghosts = lax.all_to_all(ghosts, ("section", "dp"), 0, 0, tiled=True)
    twos = twos[:1] + [tie(piece, ghosts) for piece in twos[1:]]
    twos = twos + [twos_own] + [swap(piece, "section", copies) for piece in twos[1:]]
    states = states_far[:1] + [tie(piece, ghosts) for piece in states_far[1:]]
    states = states + [swap(piece, "section", copies) for piece in states]
    ghosts = ghosts.reshape(sections, parts, share, lanes)
    bound = 0.8 * math.sqrt(sections * (rows // users) * width * width)

    grad_in, grad_out, weights = call(
        functools.partial(grads_kernel, rows, users, bound, copies),
        [((1, slab, rank), F32), ((1, rank, slab), F32), ((users, micro), F32)],
        [VMEM] + [FAR] * (2 * count + 1) + [ANY] * (count - 1) + [VMEM] * 2,
        limit=LIMIT + 3 * count * (states[0].size + slices.size),
        scratch_shapes=[
            pltpu.VMEM((count, parts, own, slab), BF16),
            pltpu.VMEM((count, parts, own, slab), BF16),
            pltpu.VMEM((count,) + states[0].shape, BF16),
            pltpu.VMEM((micro, lanes), F32),
            pltpu.VMEM((2 * rank, slab + (layers - 1) * rank), F32),
            pltpu.VMEM((rank, slab + layers * rank), F32),
            pltpu.SemaphoreType.DMA((count, 5)),
        ],
    )(
        *in_vmem(packs),
        *in_hbm(*ones, *twos, states[0]),
        *states[1:],
        ghosts,
        included.T,
    )
    return (grad_in, grad_out, weights.T)


def solution(mesh):
    placed = (
        P(None, "dp", None),
        P(None, "dp", None),
        P("section", "dp", None),
        P("section", None, "dp"),
        P("section", "dp"),
        P(None, "dp"),
        P(None, "dp"),
    )
    return jax.shard_map(
        shards,
        mesh=mesh,
        in_specs=placed,
        out_specs=(P("section", "dp", None), P("section", None, "dp"), P(None, "dp")),
        check_vma=False,
    )
```

```python
import functools
import math

import jax
import jax.numpy as jnp
from jax import lax
from jax.experimental import pallas as pl
from jax.experimental.pallas import tpu as pltpu
from jax.sharding import PartitionSpec as P

F32 = jnp.float32
BF16 = jnp.bfloat16
VMEM = pl.BlockSpec(memory_space=pltpu.VMEM)
SMEM = pl.BlockSpec(memory_space=pltpu.SMEM)
FAR = pl.BlockSpec(memory_space=pltpu.HBM)
ANY = pl.BlockSpec(memory_space=pl.ANY)
LIMIT = 16 * 1024 * 1024
LANES = 128
PAD = 16


def dot(left, right):
    return jnp.dot(left.astype(BF16), right.astype(BF16), preferred_element_type=F32)


def dot_last(left, right):
    return lax.dot_general(
        left.astype(BF16), right.astype(BF16), (((1,), (1,)), ((), ())), preferred_element_type=F32
    )


def dot_first(left, right):
    return lax.dot_general(
        left.astype(BF16), right.astype(BF16), (((0,), (0,)), ((), ())), preferred_element_type=F32
    )


def swap(block, axis, bit):
    size = lax.axis_size(axis)
    return lax.ppermute(block, axis, [(i, i ^ bit) for i in range(size)])


def exchange(blocks):
    return lax.all_to_all(blocks, "dp", 0, 0, tiled=True)


def out_in_vmem(shape, dtype):
    return pltpu.VMEM(shape, dtype)


def call(body, outs, specs, pinned=(), limit=LIMIT, **options):
    return pl.pallas_call(
        body,
        out_shape=[
            out_in_vmem(*out) if i in pinned else jax.ShapeDtypeStruct(*out)
            for i, out in enumerate(outs)
        ],
        in_specs=specs,
        out_specs=options.pop("out_specs", [VMEM] * len(outs)),
        compiler_params=pltpu.CompilerParams(vmem_limit_bytes=limit),
        **options,
    )


def in_hbm(*arrays):
    return [pltpu.with_memory_space_constraint(array, pltpu.HBM) for array in arrays]


def in_vmem(*arrays):
    return [pltpu.with_memory_space_constraint(array, pltpu.VMEM) for array in arrays]


def down_of(packs, layer, slab):
    return packs[layer, slab : 2 * slab, :]


def unchunk(block):
    rank = block.shape[1]
    return jnp.concatenate(
        [block[c * rank : (c + 1) * rank] for c in range(block.shape[0] // rank)], 1
    )


def up_of(packs, layer, slab):
    return unchunk(packs[layer, :slab, :])


def gain_of(packs, layer, slab):
    rank = packs.shape[2]
    rows = packs[layer, 2 * slab : 2 * slab + PAD, :].astype(F32)
    return jnp.concatenate([rows[c : c + 1, :] for c in range(slab // rank)], 1)


def first_micro(copies, share):
    return (lax.axis_index("section") // copies) * share


def split_kernel(copies, h_ref, c_ref, out_ref, sems):
    parts, _, own, slab = out_ref.shape
    rows = h_ref.shape[1]
    share = own // rows
    first = first_micro(copies, share)
    copies = []
    for i, whole in enumerate((h_ref, c_ref)):
        for n in range(parts):
            for m in range(share):
                copy = pltpu.make_async_copy(
                    whole.at[first + m, :, pl.ds(n * slab, slab)],
                    out_ref.at[n, i, pl.ds(m * rows, rows), :],
                    sems.at[i, n, m],
                )
                copy.start()
                copies.append(copy)
    for copy in copies:
        copy.wait()


def pack_kernel(down_ref, up_ref, gain_ref, up_out, down_out):
    slab, rank = down_ref.shape[1:]
    gain = gain_ref[...].astype(F32)
    parts = [gain[:, c * rank : (c + 1) * rank] for c in range(slab // rank)]
    for c, row in enumerate(parts):
        here = slice(c * rank, (c + 1) * rank)
        column = jnp.broadcast_to(row, (rank, rank)).T
        up_out[here, :] = up_ref[0, :, here]
        down_out[here, :] = (down_ref[0, here, :].astype(F32) * column).astype(BF16)
    spare = [jnp.zeros((PAD - len(parts), rank), F32)]
    down_out[slab:, :] = jnp.concatenate(parts + spare, 0).astype(BF16)


def products_kernel(down_ref, *refs):
    *pieces, gram_ref, ups_ref, sems = refs
    sections, slab, _ = ups_ref.shape
    rank = down_ref.shape[1]
    section = lax.axis_index("section")
    copies = [
        pltpu.make_async_copy(piece, ups_ref.at[section ^ offset], sems.at[i])
        for i, (piece, offset) in enumerate(zip(pieces, gathered_offsets(sections)))
    ]
    for copy in copies:
        copy.start()
    for copy in copies:
        copy.wait()
    own = unchunk(ups_ref[section])
    down = down_ref[:slab, :]
    for j in range(sections - 1):
        up = unchunk(ups_ref[j])
        value = jnp.where(j < section, dot(up, down), dot_last(own, up))
        gram_ref[j * rank : (j + 1) * rank, :] = value.astype(BF16)


def packs_kernel(*refs):
    *pieces, packs_ref, token_ref, sems = refs
    section = lax.axis_index("section")
    sections = packs_ref.shape[0]
    copies = []
    for i, offset in enumerate(gathered_offsets(sections)):
        begin = 0
        for j in range(2):
            piece = pieces[j * sections + i]
            target = packs_ref.at[section ^ offset, pl.ds(begin, piece.shape[0]), :]
            copies.append(pltpu.make_async_copy(piece, target, sems.at[j, i]))
            begin += piece.shape[0]
    for copy in copies:
        copy.start()
    token_ref[...] = jnp.zeros_like(token_ref)
    for copy in copies:
        copy.wait()


def gathered_offsets(sections, lowest=1):
    offsets = [0]
    bit = sections // 2
    while bit >= lowest:
        offsets = offsets + [offset ^ bit for offset in offsets]
        bit //= 2
    return offsets


def gather(block, lowest=1):
    pieces = gather_far(block, lowest)
    return pieces + [swap(piece, "section", lowest) for piece in pieces]


def gather_far(block, lowest):
    pieces = [block]
    bit = lax.axis_size("section") // 2
    while bit > lowest:
        pieces = pieces + [swap(piece, "section", bit) for piece in pieces]
        bit //= 2
    return pieces


def tie_kernel(block_ref, _, out_ref):
    del block_ref, out_ref


def tie(block, after):
    return call(
        tie_kernel,
        [(block.shape, block.dtype)],
        [ANY] * 2,
        out_specs=[ANY],
        input_output_aliases={0: 0},
    )(block, after)[0]


def notes_kernel(
    copies, slices_ref, h_ref, users_ref, included_ref, _, one_ref, two_ref, notes_far, h_held, notes_ref, sems
):
    share, rows, _ = h_held.shape
    users = included_ref.shape[1]
    first = first_micro(copies, share)
    copy = pltpu.make_async_copy(h_ref.at[pl.ds(first, share)], h_held, sems.at[0])
    copy.start()
    cut, others = one_ref.shape[0], two_ref.shape[0]
    leaving = [
        pltpu.make_async_copy(slices_ref.at[pl.ds(0, cut)], one_ref, sems.at[1]),
        pltpu.make_async_copy(slices_ref.at[pl.ds(cut, others)], two_ref, sems.at[2]),
    ]
    for move in leaving:
        move.start()
    copy.wait()
    lane = lax.broadcasted_iota(jnp.int32, (rows, LANES), 1)
    diagonal = lax.broadcasted_iota(jnp.int32, (rows, rows), 0) == lax.broadcasted_iota(
        jnp.int32, (rows, rows), 1
    )
    for m in range(share):
        ids = users_ref[pl.ds(first + m, 1), :] - lax.axis_index("dp") * users
        column = jnp.sum(jnp.where(diagonal, ids, 0), -1, keepdims=True)
        wanted = included_ref[pl.ds(first + m, 1), :]
        chosen = jnp.zeros((rows, 1), jnp.int32)
        for u in range(users):
            chosen = chosen + jnp.where(column == u, wanted[:, u : u + 1], 0)
        wide = h_held[m].astype(F32)
        square = jnp.sum(wide * wide, -1, keepdims=True)
        notes = jnp.where(lane == 0, column.astype(F32), 0.0)
        notes = jnp.where(lane == 1, chosen.astype(F32), notes)
        notes_ref[m * rows : (m + 1) * rows, :] = jnp.where(lane == 2, square, notes)
    leaving.append(pltpu.make_async_copy(notes_ref, notes_far, sems.at[3]))
    leaving[-1].start()
    for move in leaving:
        move.wait()


def add_far_kernel(one_ref, two_ref, out_ref, held_ref, sem):
    held_ref[...] = (one_ref[...].astype(F32) + two_ref[...].astype(F32)).astype(BF16)
    copy = pltpu.make_async_copy(held_ref, out_ref, sem)
    copy.start()
    copy.wait()


def add_kernel(one_ref, two_ref, _, out_ref):
    out_ref[...] = (one_ref[...].astype(F32) + two_ref[...].astype(F32)).astype(BF16)


def project_kernel(slices_ref, packs_ref, _, out_ref, token_ref, held_ref, sems):
    token_ref[...] = jnp.zeros_like(token_ref)
    parts, _, own, slab = slices_ref.shape
    sections, _, rank = packs_ref.shape
    slice_h = slices_ref[:, 0].reshape(parts * own, slab)
    slice_c = slices_ref[:, 1].reshape(parts * own, slab)

    leaving = []

    def put(value, index):
        here = pl.ds(index * own, own)
        held_ref[:, here, :] = value.astype(BF16).reshape(parts, own, rank)
        leaving.append(
            pltpu.make_async_copy(held_ref.at[:, here, :], out_ref.at[:, here, :], sems.at[index])
        )
        leaving[-1].start()

    for l in range(sections):
        put(dot(slice_h, down_of(packs_ref, l, slab)), l)
    for l in range(sections):
        up = up_of(packs_ref, l, slab)
        put(dot_last(slice_c, up), 2 * sections - 1 + l)
        if l < sections - 1:
            put(dot_last(slice_h, up), sections + l)
    for move in leaving:
        move.wait()


def solve_kernel(width, notes_far, payload_ref, *refs):
    *pieces, out_ref, gram_ref, notes_ref, held_ref, sems, out_sems = refs
    own = notes_ref.shape[0]
    parts, size, rank = out_ref.shape
    layers = (size // own - 1) // 2
    pieces = pieces[-layers:]
    each = gram_ref.shape[0] // layers
    section = lax.axis_index("section")
    copies = [pltpu.make_async_copy(notes_far, notes_ref, sems.at[layers])]
    for i, (piece, offset) in enumerate(zip(pieces, gathered_offsets(layers))):
        begin = pl.multiple_of((section ^ offset) * each, each)
        copies.append(pltpu.make_async_copy(piece, gram_ref.at[pl.ds(begin, each), :], sems.at[i]))
    for copy in copies:
        copy.start()
    def column(index):
        return jnp.sum(payload_ref[:, index * own : (index + 1) * own, :].astype(F32), 0)

    leaving = []

    def put(value, index):
        here = pl.ds(index * own, own)
        held_ref[:, here, :] = jnp.broadcast_to(value[None], (parts, own, rank))
        leaving.append(
            pltpu.make_async_copy(held_ref.at[:, here, :], out_ref.at[:, here, :], out_sems.at[index])
        )
        leaving[-1].start()

    p = [column(i) for i in range(layers)]
    through = [column(layers + i) for i in range(layers - 1)]
    e = [column(2 * layers - 1 + i) for i in range(layers)]
    for copy in copies:
        copy.wait()
    gram = [
        [gram_ref[s * each + j * rank : s * each + (j + 1) * rank, :] for j in range(layers - 1)]
        for s in range(layers)
    ]
    square = notes_ref[:, 2:3]
    seen, low, exact, scale = [], [], [], []
    for l in range(layers):
        seen.append(list(through))
        scale.append(lax.rsqrt(jnp.maximum(square, 0.0) / width + 1e-05))
        exact.append(scale[l] * p[l])
        low.append(exact[l].astype(BF16))
        if l == layers - 1:
            break
        for k in range(l + 1, layers):
            p[k] = p[k] + dot(low[l], gram[k][l])
        before = through[l]
        for k in range(layers - 1):
            if k >= l:
                through[k] = through[k] + dot(low[l], gram[l][k])
            else:
                through[k] = through[k] + dot_last(low[l], gram[k][l])
        square = square + jnp.sum(low[l].astype(F32) * (before + through[l]), -1, keepdims=True)
    lane = lax.broadcasted_iota(jnp.int32, (own, rank), 1)
    extra = jnp.where(lane == 2 * layers, notes_ref[:, :1], 0.0)
    extra = jnp.where(lane == 2 * layers + 1, notes_ref[:, 1:2], extra)
    for l in range(layers - 1, -1, -1):
        err = e[l]
        mean = jnp.sum(err * exact[l], -1, keepdims=True) / width
        alpha = scale[l] * scale[l] * mean
        scaled = (scale[l] * err).astype(BF16)
        for k in range(l):
            e[k] = e[k] + dot_last(scaled, gram[l][k]) - alpha * seen[l][k]
        put(low[l], l)
        put(scaled, layers + l)
        coarse = alpha.astype(BF16).astype(F32)
        extra = jnp.where(lane == l, coarse, extra)
        extra = jnp.where(lane == layers + l, alpha - coarse, extra)
    put(extra.astype(BF16), 2 * layers)
    for move in leaving:
        move.wait()


def spread(extra, columns):
    rank = extra.shape[1]
    row = lax.broadcasted_iota(jnp.int32, (rank, rank), 0)
    picks = []
    for column in columns:
        pick = row == column[0]
        for other in column[1:]:
            pick = pick | (row == other)
        picks.append(jnp.where(pick, 1.0, 0.0).astype(BF16))
    wide = dot(extra, jnp.concatenate(picks, 1))
    return [wide[:, i * rank : (i + 1) * rank] for i in range(len(columns))]


def tiled(block, width):
    return jnp.concatenate([block] * (width // block.shape[1]), 1)


def place_of(counts, dimension, lanes):
    rows = math.prod(counts)
    return lax.broadcasted_iota(jnp.int32, counts + (lanes,), dimension).reshape(rows, lanes)


def user_lanes(ids, counts, users, lanes, m):
    lane = lax.broadcasted_iota(jnp.int32, (ids.shape[0], lanes), 1)
    user = tiled(ids, lanes).astype(jnp.int32) + place_of(counts, 0, lanes) * users
    mine = lane == user
    return mine if counts[1] == 1 else mine & (place_of(counts, 1, lanes) == m)


def state_rows(ref, index, own):
    parts, _, rank = ref.shape
    return ref[:, index * own : (index + 1) * own, :].reshape(parts * own, rank)


def streams_kernel(
    rows, users, slices_ref, packs_ref, states_ref, ghosts_ref, streams_ref, held_ref, sems
):
    parts, _, own, slab = slices_ref.shape
    layers, _, rank = packs_ref.shape
    everyone = parts * own
    counts = (parts, own // rows, rows)
    halves = [pl.ds(0, layers * own), pl.ds(layers * own, (layers + 1) * own)]
    copies = [
        pltpu.make_async_copy(states_ref.at[:, half], held_ref.at[:, half], sems.at[i])
        for i, half in enumerate(halves)
    ]
    for copy in copies:
        copy.start()

    def state(index):
        return state_rows(held_ref, index, own)

    step = rows
    while step < 256 and everyone % (2 * step) == 0:
        step *= 2
    spans = [slice(at, at + step) for at in range(0, everyone, step)]
    pairs = [jnp.zeros((step, step), F32) for _ in spans]
    stream = slices_ref[:, 0].reshape(everyone, slab)
    wide = stream.astype(F32)
    for l in range(layers):
        streams_ref[l] = stream
        normed = (wide * gain_of(packs_ref, l, slab)).astype(BF16)
        grams = [dot_last(normed[here], normed[here]) for here in spans]
        if l == 0:
            for copy in copies:
                copy.wait()
        low, scaled = state(l), state(layers + l)
        for at, here in enumerate(spans):
            pairs[at] += grams[at] * dot_last(scaled[here], scaled[here])
        if l < layers - 1:
            wide = wide + dot(low, up_of(packs_ref, l, slab))
            stream = wide.astype(BF16)
    extra = state(2 * layers)
    columns = [(2 * layers,)] + [(l, layers + l) for l in range(1, layers)]
    ids, *alphas = spread(extra, columns)
    delta = slices_ref[:, 1].reshape(everyone, slab)
    wide = delta.astype(F32)
    for l in range(layers - 1, -1, -1):
        low = state(l)
        for at, here in enumerate(spans):
            pairs[at] += dot_last(low[here], low[here]) * dot_last(delta[here], delta[here])
        if l > 0:
            wide = wide + dot_last(state(layers + l), down_of(packs_ref, l, slab))
            wide = wide - tiled(alphas[l - 1], slab) * streams_ref[l].astype(F32)
            delta = wide.astype(BF16)
    block = place_of((everyone // rows, rows), 0, rank).astype(F32)
    numbers = ids + block * users
    rowsums = []
    for at, here in enumerate(spans):
        number = numbers[here]
        other = jnp.transpose(number)[:1, :]
        own_number = tiled(number, step) if step >= rank else number[:, :step]
        rowsums.append(
            jnp.sum(jnp.where(own_number == other, pairs[at], 0.0), -1, keepdims=True)
        )
    rowsum = jnp.concatenate(rowsums, 0)
    copies, share, lanes = ghosts_ref.shape
    for m in range(share):
        mine = user_lanes(ids, counts, users, lanes, m)
        total = jnp.sum(jnp.where(mine, rowsum, 0.0), 0, keepdims=True)
        ghosts_ref[:, m : m + 1, :] = jnp.broadcast_to(total[None], (copies, 1, lanes))

def grads_kernel(rows, users, bound, copies, packs_ref, *refs):
    count = (len(refs) - 12) // 3
    one_pieces, two_pieces, state_pieces = (refs[i * count : (i + 1) * count] for i in range(3))
    (
        ghosts_ref,
        included_ref,
        in_ref,
        out_ref,
        weights_ref,
        h_held,
        c_held,
        state_held,
        clips_ref,
        h_sum,
        c_sum,
        sems,
    ) = refs[3 * count :]
    layers, _, rank = packs_ref.shape
    _, parts, own, slab = h_held.shape
    cut = one_pieces[0].shape[0]
    everyone = parts * own
    share, lanes = ghosts_ref.shape[2:]
    section = lax.axis_index("section")
    offsets = gathered_offsets(layers, copies)

    def moves(at, entry):
        one, two = pl.ds(0, cut), pl.ds(cut, parts - cut)
        return [
            pltpu.make_async_copy(state_pieces[entry], state_held.at[at], sems.at[at, 0]),
            pltpu.make_async_copy(one_pieces[entry].at[:, 0], h_held.at[at, one], sems.at[at, 1]),
            pltpu.make_async_copy(two_pieces[entry].at[:, 0], h_held.at[at, two], sems.at[at, 2]),
            pltpu.make_async_copy(one_pieces[entry].at[:, 1], c_held.at[at, one], sems.at[at, 3]),
            pltpu.make_async_copy(two_pieces[entry].at[:, 1], c_held.at[at, two], sems.at[at, 4]),
        ]

    for entry in range(count):
        for move in moves(entry, entry):
            move.start()
    h_sum[...] = jnp.zeros_like(h_sum)
    c_sum[...] = jnp.zeros_like(c_sum)
    columns = [(2 * layers,), (2 * layers + 1,)]
    for k in range(1, layers):
        taken = [jnp.where(l > section, l, -1) for l in range(k, layers)]
        columns.append(taken + [jnp.where(l >= 0, layers + l, -1) for l in taken])
    group = max(1, min(count, 512 // everyone))

    @pl.loop(0, count // group)
    def _(step):
        begin = step * group
        scaled, low, rest = [], [], [[] for _ in range(layers - 1)]
        for i in range(group):
            at = begin + i
            for move in moves(at, 0):
                move.wait()
            offset = sum(jnp.where(at == n, value, 0) for n, value in enumerate(offsets))
            there = section ^ offset
            totals = sum(ghosts_ref[there, n] for n in range(parts))
            clips = bound / jnp.maximum(jnp.sqrt(totals), bound)
            clips_ref[pl.ds((there // copies) * share, share), :] = clips
            state_ref = state_held.at[at]
            ids, included, *alphas = spread(state_rows(state_ref, 2 * layers, own), columns)
            weight = jnp.zeros((everyone, 1), F32)
            for m in range(share):
                mine = user_lanes(ids, (parts, share, rows), users, lanes, m)
                weight += jnp.sum(jnp.where(mine, clips[m : m + 1, :], 0.0), -1, keepdims=True)
            weight = weight * included

            def weighted(index):
                first = pl.multiple_of(index * own, own)
                block = state_ref[:, pl.ds(first, own), :].reshape(everyone, rank)
                return weight * block.astype(F32)

            scaled.append(weighted(layers + section).astype(BF16))
            low.append(weighted(section))
            for k in range(layers - 1):
                rest[k].append((alphas[k] * low[i]).astype(BF16))
        here = pl.ds(begin, group)

        def everything(ref, *index):
            return ref[(here,) + index].reshape(group * everyone, -1)

        def known(index):
            return everything(state_held, slice(None), slice(index * own, (index + 1) * own))

        scaled = jnp.concatenate(scaled, 0)
        low = jnp.concatenate(low, 0).astype(BF16)
        for k in range(layers - 1):
            sides = jnp.concatenate([scaled, jnp.concatenate(rest[k], 0)], 1)
            if k == 0:
                h_sum[:, :slab] += dot_first(sides, everything(h_held))
            h_sum[:, slab + k * rank : slab + (k + 1) * rank] += dot_first(sides, known(k))
        c_sum[:, :slab] += dot_first(low, everything(c_held))
        errs = jnp.concatenate([known(layers + k) for k in range(layers)], 1)
        c_sum[:, slab:] += dot_first(low, errs)

    left, right = h_sum[:rank, :slab], c_sum[:, :slab] - h_sum[rank:, :slab]
    for k in range(layers):
        beside = slice(slab + k * rank, slab + (k + 1) * rank)
        later = (k > section).astype(F32)
        right += dot_last(later * c_sum[:, beside], down_of(packs_ref, k, slab))
        if k < layers - 1:
            up = up_of(packs_ref, k, slab)
            earlier = (k < section).astype(F32)
            left += dot(earlier * h_sum[:rank, beside], up)
            right -= dot(h_sum[rank:, beside], up)
    out_ref[0] = right
    left = left * gain_of(packs_ref, section, slab)
    for c in range(slab // rank):
        part = slice(c * rank, (c + 1) * rank)
        in_ref[0, part, :] = left[:, part].T
    users_here, micro = included_ref.shape
    mine = lax.broadcasted_iota(jnp.int32, (micro, lanes), 1) - lax.axis_index("dp") * users
    diagonal = lax.broadcasted_iota(jnp.int32, (micro, micro), 0) == lax.broadcasted_iota(
        jnp.int32, (micro, micro), 1
    )
    for u in range(users_here):
        column = jnp.sum(jnp.where(mine == u, clips_ref[...], 0.0), -1, keepdims=True)
        row = jnp.sum(jnp.where(diagonal, column, 0.0), 0, keepdims=True)
        weights_ref[u : u + 1, :] = included_ref[u : u + 1, :].astype(F32) * row


def sum_parts(value, token):
    size = lax.axis_size("dp")
    bits = [1 << i for i in range(1, size.bit_length() - 1)]
    for bit in bits:
        came = swap(value, "dp", bit)
        if bit != bits[-1]:
            value = (value.astype(F32) + came.astype(F32)).astype(BF16)
        else:
            (value,) = call(add_kernel, [(value.shape, BF16)], [VMEM] * 3)(value, came, token)
    return value, swap(value, "dp", 1)


def shards(hidden_in, cotangent, adapter_in, adapter_out, norm_gain, user_of_row, included):
    sections = lax.axis_size("section")
    section = lax.axis_index("section")
    parts = lax.axis_size("dp")
    dp_index = lax.axis_index("dp")
    micro, rows, width = hidden_in.shape
    rank = adapter_in.shape[2]
    users = included.shape[1]
    layers = sections
    slab = width // parts
    share = max(1, micro // sections)
    copies = max(1, sections // micro)
    own = share * rows
    everyone = parts * own

    up, down = call(
        pack_kernel, [((slab, rank), BF16), ((slab + PAD, rank), BF16)], [VMEM] * 3
    )(*in_hbm(adapter_in, adapter_out, norm_gain))
    ups = gather(up)
    downs = gather(down)
    (blocks,) = call(
        functools.partial(split_kernel, copies),
        [((parts, 2, own, slab), BF16)],
        [FAR, FAR],
        scratch_shapes=[pltpu.SemaphoreType.DMA((2, parts, share))],
    )(*in_hbm(hidden_in, cotangent))
    slices = exchange(blocks)

    each = (layers - 1) * rank
    (gram,) = call(
        products_kernel,
        [((each, rank), BF16)],
        [VMEM, FAR] + [ANY] * (sections - 1),
        scratch_shapes=[
            pltpu.VMEM((sections, slab, rank), BF16),
            pltpu.SemaphoreType.DMA((sections,)),
        ],
    )(down, *in_hbm(up), *ups[1:])
    packs, token = call(
        packs_kernel,
        [((sections, 2 * slab + PAD, rank), BF16), ((8, LANES), F32)],
        [FAR] * (2 * sections),
        pinned=(0,),
        scratch_shapes=[pltpu.SemaphoreType.DMA((2, sections))],
    )(*in_hbm(*ups, *downs))
    sent, came = sum_parts(gram, token)

    payload, token = call(
        project_kernel,
        [((parts, (3 * layers - 1) * own, rank), BF16), ((8, LANES), F32)],
        [VMEM, VMEM, ANY],
        out_specs=[FAR, VMEM],
        scratch_shapes=[
            pltpu.VMEM((parts, (3 * layers - 1) * own, rank), BF16),
            pltpu.SemaphoreType.DMA((3 * layers - 1,)),
        ],
    )(slices, *in_vmem(packs), sent)
    payload = exchange(payload)
    (gram,) = call(
        add_far_kernel,
        [(sent.shape, BF16)],
        [VMEM] * 2,
        out_specs=[FAR],
        scratch_shapes=[pltpu.VMEM(sent.shape, BF16), pltpu.SemaphoreType.DMA],
    )(sent, came)
    grams = gather(gram)
    cut = max(1, parts * 2 // 8)
    one, two, notes = call(
        functools.partial(notes_kernel, copies),
        [
            ((cut, 2, own, slab), BF16),
            ((parts - cut, 2, own, slab), BF16),
            ((own, LANES), F32),
        ],
        [VMEM, FAR, VMEM, VMEM, VMEM],
        out_specs=[FAR] * 3,
        scratch_shapes=[
            pltpu.VMEM((share, rows, width), BF16),
            pltpu.VMEM((own, LANES), F32),
            pltpu.SemaphoreType.DMA((4,)),
        ],
    )(slices, *in_hbm(hidden_in), user_of_row, included, token)
    ones = gather_far(one, copies)
    twos = gather_far(two, copies)
    ones_own, twos_own = swap(one, "section", copies), swap(two, "section", copies)
    count = 2 * len(ones)

    (state,) = call(
        functools.partial(solve_kernel, width),
        [((parts, (2 * layers + 1) * own, rank), BF16)],
        [FAR, VMEM] + [FAR] * (3 + len(grams)),
        scratch_shapes=[
            pltpu.VMEM((layers * each, rank), BF16),
            pltpu.VMEM((own, LANES), F32),
            pltpu.VMEM((parts, (2 * layers + 1) * own, rank), BF16),
            pltpu.SemaphoreType.DMA((layers + 1,)),
            pltpu.SemaphoreType.DMA((2 * layers + 1,)),
        ],
        out_specs=[FAR],
    )(*in_hbm(notes), payload, *in_hbm(ones[1], ones_own, twos_own, *grams))
    states = exchange(state)

    lanes = -(-users * parts // LANES) * LANES
    (ghosts,) = call(
        functools.partial(streams_kernel, rows, users),
        [((sections * parts, share, lanes), F32)],
        [VMEM, VMEM, FAR],
        limit=LIMIT + 4 * states.size,
        scratch_shapes=[
            pltpu.VMEM((layers, everyone, slab), BF16),
            pltpu.VMEM(states.shape, BF16),
            pltpu.SemaphoreType.DMA((2,)),
        ],
    )(slices, *in_vmem(packs), *in_hbm(states))
    states_far = gather_far(states, copies)
    ghosts = lax.all_to_all(ghosts, ("section", "dp"), 0, 0, tiled=True)
    ones = ones[:1] + [tie(piece, ghosts) for piece in ones[1:]]
    twos = twos[:1] + [tie(piece, ghosts) for piece in twos[1:]]
    ones = ones + [ones_own] + [swap(piece, "section", copies) for piece in ones[1:]]
    twos = twos + [twos_own] + [swap(piece, "section", copies) for piece in twos[1:]]
    states = states_far[:1] + [tie(piece, ghosts) for piece in states_far[1:]]
    states = states + [swap(piece, "section", copies) for piece in states]
    ghosts = ghosts.reshape(sections, parts, share, lanes)
    bound = 0.8 * math.sqrt(sections * (rows // users) * width * width)

    grad_in, grad_out, weights = call(
        functools.partial(grads_kernel, rows, users, bound, copies),
        [((1, slab, rank), F32), ((1, rank, slab), F32), ((users, micro), F32)],
        [VMEM] + [FAR] * (2 * count + 1) + [ANY] * (count - 1) + [VMEM] * 2,
        limit=LIMIT + 3 * count * (states[0].size + slices.size),
        scratch_shapes=[
            pltpu.VMEM((count, parts, own, slab), BF16),
            pltpu.VMEM((count, parts, own, slab), BF16),
            pltpu.VMEM((count,) + states[0].shape, BF16),
            pltpu.VMEM((micro, lanes), F32),
            pltpu.VMEM((2 * rank, slab + (layers - 1) * rank), F32),
            pltpu.VMEM((rank, slab + layers * rank), F32),
            pltpu.SemaphoreType.DMA((count, 5)),
        ],
    )(
        *in_vmem(packs),
        *in_hbm(*ones, *twos, states[0]),
        *states[1:],
        ghosts,
        included.T,
    )
    return (grad_in, grad_out, weights.T)


def solution(mesh):
    placed = (
        P(None, "dp", None),
        P(None, "dp", None),
        P("section", "dp", None),
        P("section", None, "dp"),
        P("section", "dp"),
        P(None, "dp"),
        P(None, "dp"),
    )
    return jax.shard_map(
        shards,
        mesh=mesh,
        in_specs=placed,
        out_specs=(P("section", "dp", None), P("section", None, "dp"), P(None, "dp")),
        check_vma=False,
    )
```
